32 devices in a mesh: slides: 2 (over x), cols: 8 (over z, y), rows: 2 (over core).
Axes of the slice: x: 2, y: 2, z: 4, core: 2. Of those that a mesh axis runs over, the one named last changes fastest.
Arguments:
- pixels: bfloat16 [3, 256, 8192], P(None, 'rows', ('slides', 'cols')), parts along dimension 2, may hold values from -6 to 6
- patch_weight: bfloat16 [24, 24, 3, 768], replicated, may hold values from -0.15625 to 0.15625
- patch_bias: float32 [768], replicated, may hold values from -3 to 3
- norm_gain: float32 [768], replicated, may hold values from 0.1 to 1.9
- gate_weight: bfloat16 [768, 1536], replicated, may hold values from -0.21875 to 0.21875
- mix_weight: bfloat16 [768, 1664], replicated, may hold values from -0.21875 to 0.21875
- step_weight: bfloat16 [768, 24], replicated, may hold values from -0.21875 to 0.21875
- step_bias: float32 [24], replicated, may hold values from -5 to -2
- log_rate: float32 [24], replicated, may hold values from -11 to 2
- conv_weight: float32 [4, 1664], replicated, may hold values from -3 to 3
- conv_bias: float32 [1664], replicated, may hold values from -3 to 3
- skip_gain: float32 [24], replicated, may hold values from 0.25 to 2
- out_gain: float32 [1536], replicated, may hold values from 0.1 to 1.9
- out_weight: bfloat16 [1536, 768], replicated, may hold values from -0.15625 to 0.15625
Outputs:
- layer_out: bfloat16 [8192, 768], P(('slides', 'cols', 'rows')), parts along dimension 0
The draws below stay inside these ranges and needn't reach their ends.
There are 2 independent parts, one for each index of `slides`. The reference program is written for one: setup_inputs(seed, part) draws one part's arguments, and reference() takes and returns one part's arrays. A program takes and returns all parts, laid end to end along the dimension named above; an argument that names none is the same for every part. Nothing has to cross between parts.
All inputs are finite; a program needn't handle non-finite values.
Results may differ from the reference program's by a relative error of at most 0.011.
Values may be sent and summed in bfloat16 or wider, within the bound.
A program may use at most 192 MiB of HBM per device.

```python
from functools import partial
import jax
import jax.numpy as jnp
from jax import lax

D = 768
E = 1536
HDIM = 64
NSTATE = 64
CONVK = 4
CHAN = 3
PATCH = 16
KERNEL = 24
BAND = 256
SPAN = 256
HEADS = 24
TOKENS = 4096
WIDTH_PX = 4096


def head_rates(key):
    folded = jax.random.fold_in(key, 4242)
    key_base, key_order, key_slow, key_fast = jax.random.split(folded, 4)
    base_step = jnp.exp(jax.random.uniform(key_base, (HEADS,), jnp.float32, jnp.log(0.01), jnp.log(0.1)))
    slow_count = HEADS // 2
    ranking = jax.random.permutation(key_order, HEADS)
    slow_rate = jnp.exp(jax.random.uniform(key_slow, (HEADS,), jnp.float32, jnp.log(0.3 / TOKENS), jnp.log(1.5 / TOKENS)))
    fast_rate = jnp.exp(jax.random.uniform(key_fast, (HEADS,), jnp.float32, jnp.log(1.0 / 50.0), jnp.log(1.0 / 20.0)))
    head_rate = jnp.where(ranking < slow_count, slow_rate, fast_rate)
    return (base_step, head_rate)


def draw_step_bias(key, part):
    return jnp.log(jnp.expm1(head_rates(key)[0]))


def draw_log_rate(key, part):
    base_step, head_rate = head_rates(key)
    return jnp.log(head_rate / base_step)


def levels(own_key, extent, cuts, least, high):
    def one(position, blocks):
        steps = jax.random.uniform(jax.random.fold_in(jax.random.fold_in(own_key, 6), position), (blocks,), jnp.float32, least / len(cuts), high / len(cuts))
        return jnp.repeat(jnp.exp(steps), extent[position] // blocks).reshape((-1,) + (1,) * (len(extent) - position - 1))

    level = one(*cuts[0])
    for cut in cuts[1:]:
        level = level * one(*cut)
    return level


def noise(rng, dims, spread, reach, shards=(), held_as=jnp.bfloat16):
    values = spread * jax.random.normal(rng, dims, jnp.float32)
    if shards:
        values = values * levels(rng, dims, shards, -0.22, 0.18)
    return jnp.clip(values, -reach, reach).astype(held_as)


def setup_inputs(seed: int = 0, part: int = 0) -> dict:
    keys = jax.random.split(jax.random.key(seed), 15)
    part_splits = jax.random.split(jax.random.fold_in(keys[14], part), 15)
    pixels = noise(part_splits[0], (CHAN, BAND, WIDTH_PX), 1.0, 6.0, ((1, 2), (2, 8)))
    patch_weight = noise(keys[1], (KERNEL, KERNEL, CHAN, D), (KERNEL * KERNEL * CHAN) ** -0.5, 0.15625)
    patch_bias = noise(keys[2], (D,), 0.5, 3.0, (), jnp.float32)
    norm_gain = jnp.clip(1.0 + 0.18 * jax.random.normal(keys[3], (D,), jnp.float32), 0.1, 1.9)
    gate_weight = noise(keys[4], (D, E), D ** -0.5, 0.21875)
    mix_weight = noise(keys[5], (D, E + 2 * NSTATE), D ** -0.5, 0.21875)
    step_weight = noise(keys[6], (D, HEADS), D ** -0.5, 0.21875)
    step_bias = draw_step_bias(jax.random.fold_in(keys[14], 71), part)
    log_rate = draw_log_rate(jax.random.fold_in(keys[14], 71), part)
    conv_weight = noise(keys[9], (CONVK, E + 2 * NSTATE), CONVK ** -0.5, 3.0, (), jnp.float32)
    conv_bias = noise(keys[10], (E + 2 * NSTATE,), 0.5, 3.0, (), jnp.float32)
    skip_gain = jnp.clip(jax.random.uniform(keys[11], (HEADS,), jnp.float32, 0.25, 2.0), 0.25, 2.0)
    out_gain = jnp.clip(1.0 + 0.18 * jax.random.normal(keys[12], (E,), jnp.float32), 0.1, 1.9)
    out_weight = noise(keys[13], (E, D), E ** -0.5, 0.15625)
    return dict(pixels=pixels, patch_weight=patch_weight, patch_bias=patch_bias, norm_gain=norm_gain, gate_weight=gate_weight, mix_weight=mix_weight, step_weight=step_weight, step_bias=step_bias, log_rate=log_rate, conv_weight=conv_weight, conv_bias=conv_bias, skip_gain=skip_gain, out_gain=out_gain, out_weight=out_weight)


def rms_scale(values, gains):
    mean_sq = lax.optimization_barrier(jnp.mean(values * values, axis=-1, keepdims=True))
    return values * lax.rsqrt(mean_sq + 1e-05) * gains.astype(jnp.float32)

def block_step(carry_state, pieces, skip_vec):
    head_in, b_mat, c_mat, step_size, log_decay = pieces
    cum_decay = jnp.cumsum(log_decay, axis=0)
    scores = jnp.dot(c_mat, b_mat.T, preferred_element_type=jnp.float32)
    cum_heads = cum_decay.T
    decay_gap = cum_heads[:, :, None] - cum_heads[:, None, :]
    causal = jnp.arange(SPAN)[:, None] >= jnp.arange(SPAN)[None, :]
    decay_w = jnp.where(causal, jnp.exp(jnp.where(causal, decay_gap, 0.0)), 0.0)
    weights = (scores[None] * decay_w * step_size.T[:, None, :]).astype(jnp.bfloat16)
    inputs_f = head_in.astype(jnp.float32)
    y_intra = jnp.einsum('hts,shp->thp', weights.astype(jnp.float32), inputs_f)
    y_state = jnp.exp(cum_decay)[:, :, None] * jnp.einsum('hpn,tn->thp', carry_state, c_mat.astype(jnp.float32), precision=lax.Precision.HIGHEST)
    to_end = jnp.exp(cum_decay[-1:] - cum_decay) * step_size
    fresh_state = jnp.einsum('thp,tn->hpn', inputs_f * to_end[:, :, None], b_mat.astype(jnp.float32), precision=lax.Precision.HIGHEST)
    next_state = jnp.exp(cum_decay[-1])[:, None, None] * carry_state + fresh_state
    result = y_intra + y_state + skip_vec[None, :, None] * inputs_f
    return (next_state, result)

def reference(pixels, patch_weight, patch_bias, norm_gain, gate_weight, mix_weight, step_weight, step_bias, log_rate, conv_weight, conv_bias, skip_gain, out_gain, out_weight):
    margin = (KERNEL - PATCH) // 2
    embed_grid = lax.conv_general_dilated(pixels[None], patch_weight, (PATCH, PATCH), ((margin, margin), (margin, margin)), dimension_numbers=('NCHW', 'HWIO', 'NHWC'), preferred_element_type=jnp.float32)[0]
    embedded = (embed_grid + patch_bias.astype(jnp.float32)).astype(jnp.bfloat16).reshape(TOKENS, D)
    resid = embedded.astype(jnp.float32)
    normed = rms_scale(resid, norm_gain).astype(jnp.bfloat16)
    gate_proj = jnp.dot(normed, gate_weight, preferred_element_type=jnp.float32).astype(jnp.bfloat16)
    mixed_raw = jnp.dot(normed, mix_weight, preferred_element_type=jnp.float32).astype(jnp.bfloat16)
    step_raw = jnp.dot(normed, step_weight, preferred_element_type=jnp.float32)
    window = jnp.concatenate([jnp.zeros((CONVK - 1, E + 2 * NSTATE), jnp.bfloat16), mixed_raw], 0).astype(jnp.float32)
    conv_sum = conv_bias.astype(jnp.float32)
    for offset in range(CONVK):
        conv_sum = conv_sum + conv_weight[offset].astype(jnp.float32) * window[offset:offset + TOKENS]
    mixed = jax.nn.silu(conv_sum).astype(jnp.bfloat16)
    step_size = jax.nn.softplus(step_raw + step_bias.astype(jnp.float32))
    log_decay = -step_size * jnp.exp(log_rate.astype(jnp.float32))
    blocks = TOKENS // SPAN
    head_in = mixed[:, :E].reshape(blocks, SPAN, HEADS, HDIM)
    b_mat = mixed[:, E:E + NSTATE].reshape(blocks, SPAN, NSTATE)
    c_mat = mixed[:, E + NSTATE:].reshape(blocks, SPAN, NSTATE)
    start_state = jnp.zeros((HEADS, HDIM, NSTATE), jnp.float32)
    stepper = partial(block_step, skip_vec=skip_gain.astype(jnp.float32))
    unused_state, head_out = lax.scan(stepper, start_state, (head_in, b_mat, c_mat, step_size.reshape(blocks, SPAN, HEADS), log_decay.reshape(blocks, SPAN, HEADS)))
    gated = head_out.reshape(TOKENS, E) * jax.nn.silu(gate_proj.astype(jnp.float32))
    hidden = rms_scale(gated, out_gain).astype(jnp.bfloat16)
    return (jnp.dot(hidden, out_weight, preferred_element_type=jnp.float32) + resid).astype(jnp.bfloat16)
```

```python
import functools

import jax
import jax.numpy as jnp
from jax import lax
from jax.experimental import pallas as pl
from jax.experimental.pallas import tpu as pltpu
from jax.sharding import PartitionSpec as P

E = 1536
HDIM = 64
NSTATE = 64
PATCH = 16
KERNEL = 24
SPAN = 256
HEADS = 24


F32 = jnp.float32
BF16 = jnp.bfloat16
CHAN = 3
LEAD = 16
WIN = 80
OWN_AT = 16 + 256 + 16
HI = lax.Precision.HIGHEST


def layer_kernel(
    dims, x_ref, wp_hbm, mix_hbm, gate_hbm, out_hbm, step_ref, small_ref, o_ref,
    wp, mixw, gatew, outw, w_sem,
    recv, recv_prev, recv_next, trans, patches, emb, normed, raw, mixed, gate, yacc, xw,
    squart, squart_in, logs, tot_out, tot_in, inc_out, inc_in, inc_acc,
    x_send, x_prev_send, x_next_send, x_recv, prev_recv, next_recv,
    q_send, q_recv, l_send, l_recv, t_send, t_recv, i_send, i_recv,
):
    cols, nr, local_rows, width = dims
    ndev = cols * nr
    parts = ndev // (local_rows * nr)
    per_part = cols // parts
    ngroup = ndev // 4
    d_model = emb.shape[1]
    c = lax.axis_index("cols")
    r = lax.axis_index("rows")
    me = c * nr + r
    e = lax.rem(me, 4)
    g = me // 4

    def dev(index):
        return {"cols": index // nr, "rows": lax.rem(index, nr)}

    loads = [
        pltpu.make_async_copy(s, t, w_sem.at[n])
        for n, (s, t) in enumerate(
            ((wp_hbm, wp), (mix_hbm, mixw), (gate_hbm, gatew), (out_hbm, outw))
        )
    ]
    for load in loads:
        load.start()

    barrier = pltpu.get_barrier_semaphore()
    for hop in range(1, ndev):
        pl.semaphore_signal(
            barrier, inc=1, device_id=dev(lax.rem(me + hop, ndev)),
            device_id_type=pl.DeviceIdType.MESH,
        )
    pl.semaphore_wait(barrier, ndev - 1)

    def push(cond, src, dst, send, recv_s, target):
        away = cond & (target != me)
        own = cond & (target == me)

        def remote():
            return pltpu.make_async_remote_copy(
                src, dst, send, recv_s, device_id=dev(target),
                device_id_type=pl.DeviceIdType.MESH,
            )

        @pl.when(away)
        def _():
            remote().start()

        @pl.when(own)
        def _():
            pltpu.make_async_copy(src, dst, recv_s).start()

        def done():
            @pl.when(away)
            def _():
                remote().wait_send()

        return done

    sent = []
    slot = lax.rem(c, per_part)
    part = c // per_part
    last_col = slot == per_part - 1
    first_col = (slot == 0) & (part > 0)
    quick = width - 128
    yes = r >= 0
    plan = []
    for k in range(local_rows):
        full = yes
        if k == local_rows - 1:
            full = full & (r == nr - 1)
            plan.append((k + 1, 0, WIN - 16, r < nr - 1, k))
        if k == 0:
            full = full & (r == 0)
            plan.append((k + 1, 16, WIN, r > 0, k))
        plan.append((k + 1, 0, WIN, full, k))
    plan.append((0, WIN - 16, WIN, r > 0, -1))
    plan.append((local_rows + 1, 0, 16, r < nr - 1, local_rows))
    for n, (block, lo, hi, cond, k) in enumerate(plan):
        target = (r * local_rows + k) * parts + part
        sent.append(
            push(
                cond, x_ref.at[block, pl.ds(lo, hi - lo)], recv.at[slot, pl.ds(lo, hi - lo)],
                x_send.at[n], x_recv.at[slot], target,
            )
        )
        nxt = target + 1
        sent.append(
            push(
                cond & last_col & (nxt < ndev),
                x_ref.at[block, pl.ds(lo, hi - lo), pl.ds(quick, 128)],
                recv_prev.at[pl.ds(lo, hi - lo)],
                x_prev_send.at[n], prev_recv, nxt,
            )
        )
        if parts > 1:
            sent.append(
                push(
                    cond & first_col,
                    x_ref.at[block, pl.ds(lo, hi - lo), pl.ds(0, 128)],
                    recv_next.at[pl.ds(lo, hi - lo)],
                    x_next_send.at[n], next_recv, target - 1,
                )
            )

    trans[pl.ds(0, OWN_AT)] = jnp.zeros((OWN_AT, 128), F32)
    trans[pl.ds(OWN_AT + per_part * width, 16)] = jnp.zeros((16, 128), F32)
    pad_rows = jnp.zeros((128 - WIN, 128), F32)

    def turn(block):
        return jnp.concatenate([block.astype(F32), pad_rows], 0).T

    @pl.when(me > 0)
    def _():
        pltpu.make_async_copy(recv_prev, recv_prev, prev_recv).wait()
        trans[pl.ds(16 + 128, 128)] = turn(recv_prev[...])

    for s in range(per_part):
        pltpu.make_async_copy(recv.at[s], recv.at[s], x_recv.at[s]).wait()
        for t in range(width // 128):
            trans[pl.ds(OWN_AT + s * width + t * 128, 128)] = turn(
                recv[s, :, pl.ds(t * 128, 128)]
            )

    if parts > 1:
        place = lax.rem(me, parts)

        @pl.when(place > 0)
        def _():
            trans[pl.ds(OWN_AT - 16, 4)] = trans[pl.ds(OWN_AT, 4)]
            trans[pl.ds(OWN_AT - 4, 4)] = trans[pl.ds(OWN_AT - 20, 4)]

        @pl.when(place < parts - 1)
        def _():
            pltpu.make_async_copy(recv_next, recv_next, next_recv).wait()
            trans[pl.ds(OWN_AT + per_part * width, 16)] = turn(recv_next[...])[0:16]

    for kx in range(KERNEL):
        lanes = pl.ds(kx * 128, 128)
        patches[pl.ds(0, LEAD), lanes] = trans[pl.ds(12 + kx, LEAD, stride=PATCH), :].astype(BF16)
        patches[pl.ds(LEAD, SPAN), lanes] = trans[
            pl.ds(OWN_AT - 4 + kx, SPAN, stride=PATCH), :
        ].astype(BF16)

    loads[0].wait()
    for n in range(d_model // 256):
        cs = pl.ds(n * 256, 256)
        acc = jnp.dot(patches[...], wp[:, cs], preferred_element_type=F32)
        emb[:, cs] = (acc + small_ref[pl.ds(7, 1), cs]).astype(BF16)
    resid = emb[...].astype(F32)
    mean_sq = jnp.mean(resid * resid, axis=-1, keepdims=True)
    normed[...] = (
        resid * lax.rsqrt(mean_sq + 1e-05) * small_ref[pl.ds(7, 1), pl.ds(d_model, d_model)]
    ).astype(BF16)

    own = pl.ds(LEAD, SPAN)
    step_raw = jnp.dot(normed[own], step_ref[...], preferred_element_type=F32)
    sx = step_raw + small_ref[pl.ds(8, 1), pl.ds(0, 128)]
    step = jax.nn.softplus(sx)
    log_decay = -step * jnp.exp(small_ref[pl.ds(8, 1), pl.ds(128, 128)])
    rows_i = lax.broadcasted_iota(jnp.int32, (SPAN, SPAN), 0)
    cols_i = lax.broadcasted_iota(jnp.int32, (SPAN, SPAN), 1)
    causal = rows_i >= cols_i
    cum = jnp.dot(causal.astype(F32), log_decay, precision=HI, preferred_element_type=F32)
    cum_last = cum[SPAN - 1 : SPAN, :]
    to_end = jnp.exp(cum_last - cum) * step
    logs[me] = jnp.broadcast_to(cum_last, (8, 128))
    for hop in range(1, ndev):
        target = lax.rem(me + hop, ndev)
        sent.append(
            push(
                yes, logs.at[me], logs.at[me], l_send.at[hop], l_recv.at[hop], target
            )
        )

    loads[1].wait()
    total = mixw.shape[1]
    tiles = [(lo, min(256, total - lo)) for lo in range(0, total, 256)]
    has_prev = jnp.where(me > 0, 1.0, 0.0).astype(F32)
    for lo, size in tiles[::-1]:
        cs = pl.ds(lo, size)
        proj = jnp.dot(normed[...], mixw[:, cs], preferred_element_type=F32)
        raw[:, pl.ds(0, size)] = proj.astype(BF16).astype(F32)
        raw[pl.ds(0, LEAD), pl.ds(0, size)] = raw[pl.ds(0, LEAD), pl.ds(0, size)] * has_prev
        total_sum = small_ref[pl.ds(4, 1), cs]
        for k in range(4):
            total_sum = total_sum + small_ref[pl.ds(k, 1), cs] * raw[
                pl.ds(LEAD - 3 + k, SPAN), pl.ds(0, size)
            ]
        mixed[:, cs] = jax.nn.silu(total_sum).astype(BF16)

    bc = mixed[:, pl.ds(E, 2 * NSTATE)]
    b_mat = bc[:, :NSTATE]
    c_mat = bc[:, NSTATE:]
    low_half = lax.broadcasted_iota(jnp.int32, (SPAN, 128), 1) < HDIM

    def spread(values, p):
        return jnp.where(
            low_half,
            jnp.broadcast_to(values[:, 2 * p : 2 * p + 1], (SPAN, 128)),
            jnp.broadcast_to(values[:, 2 * p + 1 : 2 * p + 2], (SPAN, 128)),
        )

    pairs = HEADS // 2
    for p in range(pairs):
        ps = pl.ds(p * 128, 128)
        xw[:, ps] = (mixed[:, ps].astype(F32) * spread(to_end, p)).astype(BF16)
    quart = E // 4
    for q in range(4):
        fresh = lax.dot_general(
            b_mat, xw[:, pl.ds(q * quart, quart)], (((0,), (0,)), ((), ())),
            preferred_element_type=F32,
        )
        squart[q] = fresh.astype(BF16)
    first = g * 4
    for hop in range(1, 4):
        other = lax.rem(e + hop, 4)
        sent.append(
            push(
                yes, squart.at[other], squart_in.at[hop - 1], q_send.at[hop], q_recv.at[hop],
                first + other,
            )
        )

    loads[2].wait()
    for n in range(E // 256):
        cs = pl.ds(n * 256, 256)
        gate[:, cs] = jnp.dot(normed[own], gatew[:, cs], preferred_element_type=F32).astype(BF16)
    scores = lax.dot_general(
        c_mat, b_mat, (((1,), (1,)), ((), ())), preferred_element_type=F32
    )
    cum_t = cum.T
    step_t = step.T

    def inside(p):
        ps = pl.ds(p * 128, 128)
        x = mixed[:, ps]
        ys = []
        for h in (2 * p, 2 * p + 1):
            gap = cum[:, h : h + 1] - cum_t[h : h + 1, :]
            decay = jnp.exp(jnp.where(causal, gap, -1e30))
            w = (scores * decay * step_t[h : h + 1, :]).astype(BF16)
            ys.append(jnp.dot(w, x, preferred_element_type=F32))
        yacc[:, ps] = jnp.where(low_half, ys[0], ys[1]) + small_ref[pl.ds(6, 1), ps] * x.astype(F32)

    for p in range(0, 4):
        inside(p)

    for hop in range(1, ndev):
        source = lax.rem(me - hop + ndev, ndev)
        pltpu.make_async_copy(logs.at[source], logs.at[source], l_recv.at[hop]).wait()
    lanes_q = lax.broadcasted_iota(jnp.int32, (128, quart), 1) + e * quart
    pick = (lanes_q // HDIM == lax.broadcasted_iota(jnp.int32, (128, quart), 0)).astype(F32)

    def expand(tile):
        return jnp.exp(jnp.dot(tile, pick, precision=HI, preferred_element_type=F32))[0:1]

    for hop in range(1, 4):
        pltpu.make_async_copy(
            squart_in.at[hop - 1], squart_in.at[hop - 1], q_recv.at[hop]
        ).wait()
    prefix = [jnp.zeros((NSTATE, quart), F32)]
    befores = [jnp.zeros((8, 128), F32)]
    for n in range(4):
        hop = lax.rem(e - n + 4, 4)
        arrived = squart_in[jnp.maximum(hop - 1, 0)].astype(F32)
        state = jnp.where(hop == 0, squart[e].astype(F32), arrived)
        tile = logs[first + n]
        prefix.append(expand(tile) * prefix[-1] + state)
        befores.append(befores[-1] + tile)
    tot_out[...] = prefix[4].astype(BF16)
    for later in range(1, ngroup):
        sent.append(
            push(
                g < later, tot_out, tot_in.at[g], t_send.at[later], t_recv.at[g], later * 4 + e
            )
        )

    for p in range(4, pairs):
        inside(p)

    inc_acc[...] = jnp.zeros_like(inc_acc)
    for k in range(ngroup - 1):

        @pl.when(k < g)
        def _():
            pltpu.make_async_copy(tot_in.at[k], tot_in.at[k], t_recv.at[k]).wait()
            tile = logs[4 * k] + logs[4 * k + 1] + logs[4 * k + 2] + logs[4 * k + 3]
            inc_acc[...] = expand(tile) * inc_acc[...] + tot_in[k].astype(F32)

    for n in range(4):
        inc_out[n] = (expand(befores[n]) * inc_acc[...] + prefix[n]).astype(BF16)
    for hop in range(1, 4):
        other = lax.rem(e + hop, 4)
        sent.append(
            push(
                yes, inc_out.at[other], inc_in.at[hop - 1], i_send.at[hop], i_recv.at[hop],
                first + other,
            )
        )
    for hop in range(1, 4):
        pltpu.make_async_copy(inc_in.at[hop - 1], inc_in.at[hop - 1], i_recv.at[hop]).wait()

    grown = jnp.exp(cum)
    sq = jnp.zeros((SPAN, 128), F32)
    for q in range(4):
        hop = lax.rem(e - q + 4, 4)
        incoming = jnp.where(hop == 0, inc_out[e], inc_in[jnp.maximum(hop - 1, 0)])
        ystate = jnp.dot(c_mat, incoming, preferred_element_type=F32)
        for n in range(quart // 128):
            p = q * (quart // 128) + n
            ps = pl.ds(p * 128, 128)
            y = yacc[:, ps] + ystate[:, n * 128 : n * 128 + 128] * spread(grown, p)
            y = y * jax.nn.silu(gate[:, ps].astype(F32))
            yacc[:, ps] = y
            sq = sq + y * y
    scale = lax.rsqrt(jnp.sum(sq, axis=-1, keepdims=True) / E + 1e-05)
    for p in range(pairs):
        ps = pl.ds(p * 128, 128)
        xw[:, ps] = (yacc[:, ps] * scale * small_ref[pl.ds(5, 1), ps]).astype(BF16)
    loads[3].wait()
    for n in range(d_model // 256):
        cs = pl.ds(n * 256, 256)
        acc = jnp.dot(xw[...], outw[:, cs], preferred_element_type=F32)
        o_ref[:, cs] = (acc + emb[own, cs].astype(F32)).astype(BF16)
    for done in sent:
        done()


def body(
    pixels, patch_weight, patch_bias, norm_gain, gate_weight, mix_weight, step_weight, step_bias,
    log_rate, conv_weight, conv_bias, skip_gain, out_gain, out_weight,
):
    cols = lax.axis_size("cols")
    nr = lax.axis_size("rows")
    chan, height, width = pixels.shape
    local_rows = height // PATCH
    ndev = cols * nr
    parts = ndev // (local_rows * nr)
    per_part = cols // parts
    ngroup = ndev // 4
    quart = E // 4
    d_model = patch_weight.shape[3]
    margin = (KERNEL - PATCH) // 2
    padded = jnp.pad(pixels, ((0, 0), (PATCH, PATCH), (0, 0))).reshape(
        chan, local_rows + 2, PATCH, width
    )
    padded = padded.transpose(1, 0, 2, 3)
    edge = jnp.zeros((1, chan, margin, width), BF16)
    top = jnp.concatenate([edge, padded[:-1, :, PATCH - margin :]], 0)
    bottom = jnp.concatenate([padded[1:, :, :margin], edge], 0)

    def rows16(a):
        a = a.reshape(a.shape[0], chan * margin, a.shape[3])
        return jnp.pad(a, ((0, 0), (0, 16 - chan * margin), (0, 0)))

    windows = jnp.concatenate(
        [rows16(top), padded.reshape(local_rows + 2, chan * PATCH, width), rows16(bottom)], 1
    )
    pw = patch_weight.transpose(1, 2, 0, 3)
    mid = KERNEL - margin
    wp = jnp.concatenate(
        [
            rows16(pw[:, :, :margin]),
            pw[:, :, margin:mid].reshape(KERNEL, chan * PATCH, d_model),
            rows16(pw[:, :, mid:]),
            jnp.zeros((KERNEL, 128 - WIN, d_model), BF16),
        ],
        1,
    ).reshape(KERNEL * 128, d_model)
    total = mix_weight.shape[1]

    def row(*vectors):
        line = jnp.concatenate(vectors)
        return jnp.pad(line, (0, total - line.shape[0]))[None]

    room = jnp.zeros((128 - HEADS,), F32)
    small = jnp.concatenate(
        [
            conv_weight,
            row(conv_bias),
            row(out_gain),
            row(jnp.repeat(skip_gain, HDIM)),
            row(patch_bias, norm_gain),
            row(step_bias, room, log_rate, room),
            jnp.zeros((7, total), F32),
        ],
        0,
    )
    step_w = jnp.pad(step_weight, ((0, 0), (0, 128 - HEADS)))
    hbm = pl.BlockSpec(memory_space=pl.ANY)
    vmem = pl.BlockSpec(memory_space=pltpu.VMEM)
    dma = pltpu.SemaphoreType.DMA
    tok = SPAN + LEAD
    return pl.pallas_call(
        functools.partial(layer_kernel, (cols, nr, local_rows, width)),
        out_shape=jax.ShapeDtypeStruct((SPAN, d_model), BF16),
        in_specs=[vmem, hbm, hbm, hbm, hbm, vmem, vmem],
        out_specs=vmem,
        scratch_shapes=[
            pltpu.VMEM(wp.shape, BF16),
            pltpu.VMEM(mix_weight.shape, BF16),
            pltpu.VMEM(gate_weight.shape, BF16),
            pltpu.VMEM(out_weight.shape, BF16),
            dma((4,)),
            pltpu.VMEM((per_part, WIN, width), BF16),
            pltpu.VMEM((WIN, 128), BF16),
            pltpu.VMEM((WIN, 128), BF16),
            pltpu.VMEM((OWN_AT + per_part * width + 16, 128), F32),
            pltpu.VMEM((tok, KERNEL * 128), BF16),
            pltpu.VMEM((tok, d_model), BF16),
            pltpu.VMEM((tok, d_model), BF16),
            pltpu.VMEM((tok, 256), F32),
            pltpu.VMEM((SPAN, total), BF16),
            pltpu.VMEM((SPAN, E), BF16),
            pltpu.VMEM((SPAN, E), F32),
            pltpu.VMEM((SPAN, E), BF16),
            pltpu.VMEM((4, NSTATE, quart), BF16),
            pltpu.VMEM((3, NSTATE, quart), BF16),
            pltpu.VMEM((ndev, 8, 128), F32),
            pltpu.VMEM((NSTATE, quart), BF16),
            pltpu.VMEM((ngroup, NSTATE, quart), BF16),
            pltpu.VMEM((4, NSTATE, quart), BF16),
            pltpu.VMEM((3, NSTATE, quart), BF16),
            pltpu.VMEM((NSTATE, quart), F32),
            dma((local_rows + 4,)),
            dma((local_rows + 4,)),
            dma((local_rows + 4,)),
            dma((per_part,)),
            dma,
            dma,
            dma((4,)),
            dma((4,)),
            dma((ndev,)),
            dma((ndev,)),
            dma((ngroup,)),
            dma((ngroup,)),
            dma((4,)),
            dma((4,)),
        ],
        compiler_params=pltpu.CompilerParams(
            collective_id=0, has_side_effects=True, vmem_limit_bytes=56 * 1024 * 1024
        ),
    )(windows, wp, mix_weight, gate_weight, out_weight, step_w, small)


def solution(mesh):
    placed = (
        P(None, "rows", ("slides", "cols")),
        P(),
        P(),
        P(),
        P(),
        P(),
        P(),
        P(),
        P(),
        P(),
        P(),
        P(),
        P(),
        P(),
    )
    return jax.shard_map(
        body,
        mesh=mesh,
        in_specs=placed,
        out_specs=P(("slides", "cols", "rows"), None),
        check_vma=False,
    )
```

```python
import functools

import jax
import jax.numpy as jnp
from jax import lax
from jax.experimental import pallas as pl
from jax.experimental.pallas import tpu as pltpu
from jax.sharding import PartitionSpec as P

E = 1536
HDIM = 64
NSTATE = 64
PATCH = 16
KERNEL = 24
SPAN = 256
HEADS = 24


F32 = jnp.float32
BF16 = jnp.bfloat16
CHAN = 3
LEAD = 16
WIN = 80
OWN_AT = 16 + 256 + 16
HI = lax.Precision.HIGHEST


def layer_kernel(
    dims, x_ref, wp_hbm, mix_hbm, gate_hbm, out_hbm, step_ref, small_ref, o_ref,
    wp_raw, wide, wp, mixw, gatew, outw, w_sem,
    recv, recv_prev, recv_next, trans, patches, emb, normed, raw, mixed, gate, yacc, xw,
    squart, squart_in, logs, tot_out, tot_in, inc_out, inc_in, inc_acc,
    x_send, x_prev_send, x_next_send, x_recv, prev_recv, next_recv,
    q_send, q_recv, l_send, l_recv, t_send, t_recv, i_send, i_recv,
):
    cols, nr, local_rows, width = dims
    ndev = cols * nr
    parts = ndev // (local_rows * nr)
    per_part = cols // parts
    ngroup = ndev // 4
    d_model = emb.shape[1]
    c = lax.axis_index("cols")
    r = lax.axis_index("rows")
    me = c * nr + r
    e = lax.rem(me, 4)
    g = me // 4

    def dev(index):
        return {"cols": index // nr, "rows": lax.rem(index, nr)}

    loads = [
        pltpu.make_async_copy(s, t, w_sem.at[n])
        for n, (s, t) in enumerate(
            ((wp_hbm, wp_raw), (mix_hbm, mixw), (gate_hbm, gatew), (out_hbm, outw))
        )
    ]
    for load in loads:
        load.start()

    barrier = pltpu.get_barrier_semaphore()
    for hop in range(1, ndev):
        pl.semaphore_signal(
            barrier, inc=1, device_id=dev(lax.rem(me + hop, ndev)),
            device_id_type=pl.DeviceIdType.MESH,
        )
    pl.semaphore_wait(barrier, ndev - 1)

    def push(cond, src, dst, send, recv_s, target):
        away = cond & (target != me)
        own = cond & (target == me)

        def remote():
            return pltpu.make_async_remote_copy(
                src, dst, send, recv_s, device_id=dev(target),
                device_id_type=pl.DeviceIdType.MESH,
            )

        @pl.when(away)
        def _():
            remote().start()

        @pl.when(own)
        def _():
            pltpu.make_async_copy(src, dst, recv_s).start()

        def done():
            @pl.when(away)
            def _():
                remote().wait_send()

        return done

    sent = []
    yes = r >= 0
    slot = lax.rem(c, per_part)
    part = c // per_part
    last_col = slot == per_part - 1
    first_col = (slot == 0) & (part > 0)
    band = CHAN * PATCH

    def send_rows(n, cond, start, lo, size, target):
        src = x_ref.at[pl.ds(start, size)]
        sent.append(
            push(
                cond, src, recv.at[slot, pl.ds(lo, size)], x_send.at[n], x_recv.at[slot], target
            )
        )
        src = x_ref.at[pl.ds(start, size), pl.ds(width - 128, 128)]
        sent.append(
            push(
                cond & last_col & (target + 1 < ndev), src, recv_prev.at[pl.ds(lo, size)],
                x_prev_send.at[n], prev_recv, target + 1,
            )
        )
        if parts > 1:
            src = x_ref.at[pl.ds(start, size), pl.ds(0, 128)]
            sent.append(
                push(
                    cond & first_col, src, recv_next.at[pl.ds(lo, size)],
                    x_next_send.at[n], next_recv, target - 1,
                )
            )

    def holder(k):
        return (r * local_rows + k) * parts + part

    edge_low = r > 0
    edge_high = r < nr - 1
    for n in range(local_rows):
        k = lax.rem(n + c, local_rows)
        start = pl.multiple_of(k * band, 16)
        cut_low = edge_low & (k == 0)
        cut_high = edge_high & (k == local_rows - 1)
        send_rows(n, jnp.logical_not(cut_low | cut_high), start, 0, WIN, holder(k))
    send_rows(local_rows, edge_low, 16, 16, WIN - 16, holder(0))
    send_rows(
        local_rows + 1, edge_high, (local_rows - 1) * band, 0, WIN - 16, holder(local_rows - 1)
    )
    send_rows(local_rows + 2, edge_low, 16, WIN - 16, 16, holder(0) - parts)
    send_rows(
        local_rows + 3, edge_high, local_rows * band, 0, 16, holder(local_rows - 1) + parts
    )

    trans[pl.ds(0, OWN_AT)] = jnp.zeros((OWN_AT, 128), F32)
    trans[pl.ds(OWN_AT + per_part * width, 16)] = jnp.zeros((16, 128), F32)
    pad_rows = jnp.zeros((128 - WIN, 128), F32)

    lane_tiles = d_model // 128
    for n in range(lane_tiles):
        wide[n, pl.ds(0, 96)] = jnp.zeros((96, 128), F32)
        wide[n, pl.ds(96 + KERNEL * CHAN * KERNEL, 96)] = jnp.zeros((96, 128), F32)
    loads[0].wait()
    step_rows = CHAN * KERNEL

    def widen(n, _):
        at = pl.multiple_of(n * step_rows, 8)
        for t in range(lane_tiles):
            line = wp_raw[n, :, pl.ds(t * 128, 128)].astype(F32)
            wide[t, pl.ds(pl.multiple_of(96 + at, 8), step_rows)] = line
        return 0

    lax.fori_loop(0, KERNEL, widen, 0)

    def regroup(kx, _):
        at = pl.multiple_of(kx * 128, 128)
        for n in range(lane_tiles):
            part_n = wide.at[n][pl.ds(kx, WIN, stride=KERNEL), :]
            wp[pl.ds(at, WIN), pl.ds(n * 128, 128)] = part_n.astype(BF16)
        wp[pl.ds(pl.multiple_of(at + WIN, 16), 128 - WIN)] = jnp.zeros((128 - WIN, d_model), BF16)
        return 0

    lax.fori_loop(0, KERNEL, regroup, 0)

    def turn(block):
        return jnp.concatenate([block.astype(F32), pad_rows], 0).T

    @pl.when(me > 0)
    def _():
        pltpu.make_async_copy(recv_prev, recv_prev, prev_recv).wait()
        trans[pl.ds(16 + 128, 128)] = turn(recv_prev[...])

    for s in range(per_part):
        pltpu.make_async_copy(recv.at[s], recv.at[s], x_recv.at[s]).wait()
        for t in range(width // 128):
            trans[pl.ds(OWN_AT + s * width + t * 128, 128)] = turn(
                recv[s, :, pl.ds(t * 128, 128)]
            )

    if parts > 1:
        place = lax.rem(me, parts)

        @pl.when(place > 0)
        def _():
            trans[pl.ds(OWN_AT - 16, 4)] = trans[pl.ds(OWN_AT, 4)]
            trans[pl.ds(OWN_AT - 4, 4)] = trans[pl.ds(OWN_AT - 20, 4)]

        @pl.when(place < parts - 1)
        def _():
            pltpu.make_async_copy(recv_next, recv_next, next_recv).wait()
            trans[pl.ds(OWN_AT + per_part * width, 16)] = turn(recv_next[...])[0:16]

    for kx in range(KERNEL):
        lanes = pl.ds(kx * 128, 128)
        patches[pl.ds(0, LEAD), lanes] = trans[pl.ds(12 + kx, LEAD, stride=PATCH), :].astype(BF16)
        patches[pl.ds(LEAD, SPAN), lanes] = trans[
            pl.ds(OWN_AT - 4 + kx, SPAN, stride=PATCH), :
        ].astype(BF16)

    for n in range(d_model // 256):
        cs = pl.ds(n * 256, 256)
        acc = jnp.dot(patches[...], wp[:, cs], preferred_element_type=F32)
        emb[:, cs] = (acc + small_ref[pl.ds(7, 1), cs]).astype(BF16)
    resid = emb[...].astype(F32)
    mean_sq = jnp.mean(resid * resid, axis=-1, keepdims=True)
    normed[...] = (
        resid * lax.rsqrt(mean_sq + 1e-05) * small_ref[pl.ds(7, 1), pl.ds(d_model, d_model)]
    ).astype(BF16)

    own = pl.ds(LEAD, SPAN)
    step_raw = jnp.dot(normed[own], step_ref[...], preferred_element_type=F32)
    sx = step_raw + small_ref[pl.ds(8, 1), pl.ds(0, 128)]
    step = jax.nn.softplus(sx)
    log_decay = -step * jnp.exp(small_ref[pl.ds(8, 1), pl.ds(128, 128)])
    rows_i = lax.broadcasted_iota(jnp.int32, (SPAN, SPAN), 0)
    cols_i = lax.broadcasted_iota(jnp.int32, (SPAN, SPAN), 1)
    causal = rows_i >= cols_i
    cum = jnp.dot(causal.astype(F32), log_decay, precision=HI, preferred_element_type=F32)
    cum_last = cum[SPAN - 1 : SPAN, :]
    to_end = jnp.exp(cum_last - cum) * step
    logs[me] = jnp.broadcast_to(cum_last, (8, 128))
    for hop in range(1, ndev):
        target = lax.rem(me + hop, ndev)
        sent.append(
            push(
                yes, logs.at[me], logs.at[me], l_send.at[hop], l_recv.at[hop], target
            )
        )

    loads[1].wait()
    total = mixw.shape[1]
    tiles = [(lo, min(256, total - lo)) for lo in range(0, total, 256)]
    has_prev = jnp.where(me > 0, 1.0, 0.0).astype(F32)
    for lo, size in tiles[::-1]:
        cs = pl.ds(lo, size)
        proj = jnp.dot(normed[...], mixw[:, cs], preferred_element_type=F32)
        raw[:, pl.ds(0, size)] = proj.astype(BF16).astype(F32)
        raw[pl.ds(0, LEAD), pl.ds(0, size)] = raw[pl.ds(0, LEAD), pl.ds(0, size)] * has_prev
        total_sum = small_ref[pl.ds(4, 1), cs]
        for k in range(4):
            total_sum = total_sum + small_ref[pl.ds(k, 1), cs] * raw[
                pl.ds(LEAD - 3 + k, SPAN), pl.ds(0, size)
            ]
        mixed[:, cs] = jax.nn.silu(total_sum).astype(BF16)

    bc = mixed[:, pl.ds(E, 2 * NSTATE)]
    b_mat = bc[:, :NSTATE]
    c_mat = bc[:, NSTATE:]
    low_half = lax.broadcasted_iota(jnp.int32, (SPAN, 128), 1) < HDIM

    def spread(values, p):
        return jnp.where(
            low_half,
            jnp.broadcast_to(values[:, 2 * p : 2 * p + 1], (SPAN, 128)),
            jnp.broadcast_to(values[:, 2 * p + 1 : 2 * p + 2], (SPAN, 128)),
        )

    pairs = HEADS // 2
    for p in range(pairs):
        ps = pl.ds(p * 128, 128)
        xw[:, ps] = (mixed[:, ps].astype(F32) * spread(to_end, p)).astype(BF16)
    quart = E // 4
    for q in range(4):
        fresh = lax.dot_general(
            b_mat, xw[:, pl.ds(q * quart, quart)], (((0,), (0,)), ((), ())),
            preferred_element_type=F32,
        )
        squart[q] = fresh.astype(BF16)
    first = g * 4
    for hop in range(1, 4):
        other = lax.rem(e + hop, 4)
        sent.append(
            push(
                yes, squart.at[other], squart_in.at[hop - 1], q_send.at[hop], q_recv.at[hop],
                first + other,
            )
        )

    loads[2].wait()
    for n in range(E // 256):
        cs = pl.ds(n * 256, 256)
        gate[:, cs] = jnp.dot(normed[own], gatew[:, cs], preferred_element_type=F32).astype(BF16)
    scores = lax.dot_general(
        c_mat, b_mat, (((1,), (1,)), ((), ())), preferred_element_type=F32
    )
    cum_t = cum.T
    step_t = step.T

    def inside(p):
        ps = pl.ds(p * 128, 128)
        x = mixed[:, ps]
        ys = []
        for h in (2 * p, 2 * p + 1):
            gap = cum[:, h : h + 1] - cum_t[h : h + 1, :]
            decay = jnp.exp(jnp.where(causal, gap, -1e30))
            w = (scores * decay * step_t[h : h + 1, :]).astype(BF16)
            ys.append(jnp.dot(w, x, preferred_element_type=F32))
        yacc[:, ps] = jnp.where(low_half, ys[0], ys[1]) + small_ref[pl.ds(6, 1), ps] * x.astype(F32)

    for p in range(0, 4):
        inside(p)

    for hop in range(1, ndev):
        source = lax.rem(me - hop + ndev, ndev)
        pltpu.make_async_copy(logs.at[source], logs.at[source], l_recv.at[hop]).wait()
    lanes_q = lax.broadcasted_iota(jnp.int32, (128, quart), 1) + e * quart
    pick = (lanes_q // HDIM == lax.broadcasted_iota(jnp.int32, (128, quart), 0)).astype(F32)

    def expand(tile):
        return jnp.exp(jnp.dot(tile, pick, precision=HI, preferred_element_type=F32))[0:1]

    for hop in range(1, 4):
        pltpu.make_async_copy(
            squart_in.at[hop - 1], squart_in.at[hop - 1], q_recv.at[hop]
        ).wait()
    prefix = [jnp.zeros((NSTATE, quart), F32)]
    befores = [jnp.zeros((8, 128), F32)]
    for n in range(4):
        hop = lax.rem(e - n + 4, 4)
        arrived = squart_in[jnp.maximum(hop - 1, 0)].astype(F32)
        state = jnp.where(hop == 0, squart[e].astype(F32), arrived)
        tile = logs[first + n]
        prefix.append(expand(tile) * prefix[-1] + state)
        befores.append(befores[-1] + tile)
    tot_out[...] = prefix[4].astype(BF16)
    for later in range(1, ngroup):
        sent.append(
            push(
                g < later, tot_out, tot_in.at[g], t_send.at[later], t_recv.at[g], later * 4 + e
            )
        )

    for p in range(4, pairs):
        inside(p)

    inc_acc[...] = jnp.zeros_like(inc_acc)
    for k in range(ngroup - 1):

        @pl.when(k < g)
        def _():
            pltpu.make_async_copy(tot_in.at[k], tot_in.at[k], t_recv.at[k]).wait()
            tile = logs[4 * k] + logs[4 * k + 1] + logs[4 * k + 2] + logs[4 * k + 3]
            inc_acc[...] = expand(tile) * inc_acc[...] + tot_in[k].astype(F32)

    for n in range(4):
        inc_out[n] = (expand(befores[n]) * inc_acc[...] + prefix[n]).astype(BF16)
    for hop in range(1, 4):
        other = lax.rem(e + hop, 4)
        sent.append(
            push(
                yes, inc_out.at[other], inc_in.at[hop - 1], i_send.at[hop], i_recv.at[hop],
                first + other,
            )
        )
    for hop in range(1, 4):
        pltpu.make_async_copy(inc_in.at[hop - 1], inc_in.at[hop - 1], i_recv.at[hop]).wait()

    grown = jnp.exp(cum)
    sq = jnp.zeros((SPAN, 128), F32)
    for q in range(4):
        hop = lax.rem(e - q + 4, 4)
        incoming = jnp.where(hop == 0, inc_out[e], inc_in[jnp.maximum(hop - 1, 0)])
        ystate = jnp.dot(c_mat, incoming, preferred_element_type=F32)
        for n in range(quart // 128):
            p = q * (quart // 128) + n
            ps = pl.ds(p * 128, 128)
            y = yacc[:, ps] + ystate[:, n * 128 : n * 128 + 128] * spread(grown, p)
            y = y * jax.nn.silu(gate[:, ps].astype(F32))
            yacc[:, ps] = y
            sq = sq + y * y
    scale = lax.rsqrt(jnp.sum(sq, axis=-1, keepdims=True) / E + 1e-05)
    for p in range(pairs):
        ps = pl.ds(p * 128, 128)
        xw[:, ps] = (yacc[:, ps] * scale * small_ref[pl.ds(5, 1), ps]).astype(BF16)
    loads[3].wait()
    for n in range(d_model // 256):
        cs = pl.ds(n * 256, 256)
        acc = jnp.dot(xw[...], outw[:, cs], preferred_element_type=F32)
        o_ref[:, cs] = (acc + emb[own, cs].astype(F32)).astype(BF16)
    for done in sent:
        done()


def body(
    pixels, patch_weight, patch_bias, norm_gain, gate_weight, mix_weight, step_weight, step_bias,
    log_rate, conv_weight, conv_bias, skip_gain, out_gain, out_weight,
):
    cols = lax.axis_size("cols")
    nr = lax.axis_size("rows")
    chan, height, width = pixels.shape
    local_rows = height // PATCH
    ndev = cols * nr
    parts = ndev // (local_rows * nr)
    per_part = cols // parts
    ngroup = ndev // 4
    quart = E // 4
    d_model = patch_weight.shape[3]
    windows = jnp.pad(
        pixels.transpose(1, 0, 2).reshape(height * chan, width), ((16, 16), (0, 0))
    )
    wp = patch_weight.transpose(0, 2, 1, 3).reshape(KERNEL, CHAN * KERNEL, d_model)
    total = mix_weight.shape[1]

    def row(*vectors):
        line = jnp.concatenate(vectors)
        return jnp.pad(line, (0, total - line.shape[0]))[None]

    room = jnp.zeros((128 - HEADS,), F32)
    small = jnp.concatenate(
        [
            conv_weight,
            row(conv_bias),
            row(out_gain),
            row(jnp.repeat(skip_gain, HDIM)),
            row(patch_bias, norm_gain),
            row(step_bias, room, log_rate, room),
            jnp.zeros((7, total), F32),
        ],
        0,
    )
    step_w = jnp.pad(step_weight, ((0, 0), (0, 128 - HEADS)))
    hbm = pl.BlockSpec(memory_space=pl.ANY)
    vmem = pl.BlockSpec(memory_space=pltpu.VMEM)
    dma = pltpu.SemaphoreType.DMA
    tok = SPAN + LEAD
    return pl.pallas_call(
        functools.partial(layer_kernel, (cols, nr, local_rows, width)),
        out_shape=jax.ShapeDtypeStruct((SPAN, d_model), BF16),
        in_specs=[vmem, hbm, hbm, hbm, hbm, vmem, vmem],
        out_specs=vmem,
        scratch_shapes=[
            pltpu.VMEM(wp.shape, BF16),
            pltpu.VMEM((d_model // 128, 96 + KERNEL * CHAN * KERNEL + 96, 128), F32),
            pltpu.VMEM((KERNEL * 128, d_model), BF16),
            pltpu.VMEM(mix_weight.shape, BF16),
            pltpu.VMEM(gate_weight.shape, BF16),
            pltpu.VMEM(out_weight.shape, BF16),
            dma((4,)),
            pltpu.VMEM((per_part, WIN, width), BF16),
            pltpu.VMEM((WIN, 128), BF16),
            pltpu.VMEM((WIN, 128), BF16),
            pltpu.VMEM((OWN_AT + per_part * width + 16, 128), F32),
            pltpu.VMEM((tok, KERNEL * 128), BF16),
            pltpu.VMEM((tok, d_model), BF16),
            pltpu.VMEM((tok, d_model), BF16),
            pltpu.VMEM((tok, 256), F32),
            pltpu.VMEM((SPAN, total), BF16),
            pltpu.VMEM((SPAN, E), BF16),
            pltpu.VMEM((SPAN, E), F32),
            pltpu.VMEM((SPAN, E), BF16),
            pltpu.VMEM((4, NSTATE, quart), BF16),
            pltpu.VMEM((3, NSTATE, quart), BF16),
            pltpu.VMEM((ndev, 8, 128), F32),
            pltpu.VMEM((NSTATE, quart), BF16),
            pltpu.VMEM((ngroup, NSTATE, quart), BF16),
            pltpu.VMEM((4, NSTATE, quart), BF16),
            pltpu.VMEM((3, NSTATE, quart), BF16),
            pltpu.VMEM((NSTATE, quart), F32),
            dma((local_rows + 4,)),
            dma((local_rows + 4,)),
            dma((local_rows + 4,)),
            dma((per_part,)),
            dma,
            dma,
            dma((4,)),
            dma((4,)),
            dma((ndev,)),
            dma((ndev,)),
            dma((ngroup,)),
            dma((ngroup,)),
            dma((4,)),
            dma((4,)),
        ],
        compiler_params=pltpu.CompilerParams(
            collective_id=0, has_side_effects=True, vmem_limit_bytes=56 * 1024 * 1024
        ),
    )(windows, wp, mix_weight, gate_weight, out_weight, step_w, small)


def solution(mesh):
    placed = (
        P(None, "rows", ("slides", "cols")),
        P(),
        P(),
        P(),
        P(),
        P(),
        P(),
        P(),
        P(),
        P(),
        P(),
        P(),
        P(),
        P(),
    )
    return jax.shard_map(
        body,
        mesh=mesh,
        in_specs=placed,
        out_specs=P(("slides", "cols", "rows"), None),
        check_vma=False,
    )
```

```python
import functools

import jax
import jax.numpy as jnp
from jax import lax
from jax.experimental import pallas as pl
from jax.experimental.pallas import tpu as pltpu
from jax.sharding import PartitionSpec as P

E = 1536
HDIM = 64
NSTATE = 64
PATCH = 16
KERNEL = 24
SPAN = 256
HEADS = 24


F32 = jnp.float32
BF16 = jnp.bfloat16
CHAN = 3
LEAD = 16
WIN = 80
OWN_AT = 16 + 256 + 16
HI = lax.Precision.HIGHEST


def layer_kernel(
    dims, x_ref, wp_hbm, mix_hbm, gate_hbm, out_hbm, step_ref, tap_ref, conv_b_ref,
    gain_ref, skip_ref, patch_b_ref, norm_g_ref, bias_ref, rate_ref, o_ref,
    wp_raw, wide, wp, mixw, gatew, outw, w_sem,
    recv, recv_prev, recv_next, trans, patches, emb, normed, raw, mixed, gate, yacc, xw,
    squart, squart_in, logs, tot_out, tot_in, inc_out, inc_in, inc_acc,
    x_send, x_prev_send, x_next_send, x_recv, prev_recv, next_recv,
    q_send, q_recv, l_send, l_recv, t_send, t_recv, i_send, i_recv,
):
    cols, nr, local_rows, width = dims
    ndev = cols * nr
    parts = ndev // (local_rows * nr)
    per_part = cols // parts
    ngroup = ndev // 4
    d_model = emb.shape[1]
    c = lax.axis_index("cols")
    r = lax.axis_index("rows")
    me = c * nr + r
    e = lax.rem(me, 4)
    g = me // 4

    def dev(index):
        return {"cols": index // nr, "rows": lax.rem(index, nr)}

    loads = [
        pltpu.make_async_copy(s, t, w_sem.at[n])
        for n, (s, t) in enumerate(
            ((wp_hbm, wp_raw), (mix_hbm, mixw), (gate_hbm, gatew), (out_hbm, outw))
        )
    ]
    for load in loads:
        load.start()

    barrier = pltpu.get_barrier_semaphore()
    for hop in range(1, ndev):
        pl.semaphore_signal(
            barrier, inc=1, device_id=dev(lax.rem(me + hop, ndev)),
            device_id_type=pl.DeviceIdType.MESH,
        )
    pl.semaphore_wait(barrier, ndev - 1)

    def push(cond, src, dst, send, recv_s, target):
        away = cond & (target != me)
        own = cond & (target == me)

        def remote():
            return pltpu.make_async_remote_copy(
                src, dst, send, recv_s, device_id=dev(target),
                device_id_type=pl.DeviceIdType.MESH,
            )

        @pl.when(away)
        def _():
            remote().start()

        @pl.when(own)
        def _():
            pltpu.make_async_copy(src, dst, recv_s).start()

        def done():
            @pl.when(away)
            def _():
                remote().wait_send()

        return done

    sent = []
    yes = r >= 0
    slot = lax.rem(c, per_part)
    part = c // per_part
    last_col = slot == per_part - 1
    first_col = (slot == 0) & (part > 0)
    band = CHAN * PATCH

    def send_rows(n, cond, start, lo, size, target):
        src = x_ref.at[pl.ds(start, size)]
        sent.append(
            push(
                cond, src, recv.at[slot, pl.ds(lo, size)], x_send.at[n], x_recv.at[slot], target
            )
        )
        src = x_ref.at[pl.ds(start, size), pl.ds(width - 128, 128)]
        sent.append(
            push(
                cond & last_col & (target + 1 < ndev), src, recv_prev.at[pl.ds(lo, size)],
                x_prev_send.at[n], prev_recv, target + 1,
            )
        )
        if parts > 1:
            src = x_ref.at[pl.ds(start, size), pl.ds(0, 128)]
            sent.append(
                push(
                    cond & first_col, src, recv_next.at[pl.ds(lo, size)],
                    x_next_send.at[n], next_recv, target - 1,
                )
            )

    def holder(k):
        return (r * local_rows + k) * parts + part

    edge_low = r > 0
    edge_high = r < nr - 1
    for n in range(local_rows):
        k = lax.rem(n + c, local_rows)
        start = pl.multiple_of(k * band, 16)
        cut_low = edge_low & (k == 0)
        cut_high = edge_high & (k == local_rows - 1)
        send_rows(n, jnp.logical_not(cut_low | cut_high), start, 0, WIN, holder(k))
    send_rows(local_rows, edge_low, 16, 16, WIN - 16, holder(0))
    send_rows(
        local_rows + 1, edge_high, (local_rows - 1) * band, 0, WIN - 16, holder(local_rows - 1)
    )
    send_rows(local_rows + 2, edge_low, 16, WIN - 16, 16, holder(0) - parts)
    send_rows(
        local_rows + 3, edge_high, local_rows * band, 0, 16, holder(local_rows - 1) + parts
    )

    trans[pl.ds(0, OWN_AT)] = jnp.zeros((OWN_AT, 128), F32)
    trans[pl.ds(OWN_AT + per_part * width, 16)] = jnp.zeros((16, 128), F32)
    pad_rows = jnp.zeros((128 - WIN, 128), F32)

    lane_tiles = d_model // 128
    for n in range(lane_tiles):
        wide[n, pl.ds(0, 96)] = jnp.zeros((96, 128), F32)
        wide[n, pl.ds(96 + KERNEL * CHAN * KERNEL, 96)] = jnp.zeros((96, 128), F32)
    loads[0].wait()
    step_rows = CHAN * KERNEL

    def widen(n, _):
        at = pl.multiple_of(n * step_rows, 8)
        for t in range(lane_tiles):
            line = wp_raw[n, :, pl.ds(t * 128, 128)].astype(F32)
            wide[t, pl.ds(pl.multiple_of(96 + at, 8), step_rows)] = line
        return 0

    lax.fori_loop(0, KERNEL, widen, 0)

    def regroup(kx, _):
        at = pl.multiple_of(kx * 128, 128)
        for n in range(lane_tiles):
            part_n = wide.at[n][pl.ds(kx, WIN, stride=KERNEL), :]
            wp[pl.ds(at, WIN), pl.ds(n * 128, 128)] = part_n.astype(BF16)
        wp[pl.ds(pl.multiple_of(at + WIN, 16), 128 - WIN)] = jnp.zeros((128 - WIN, d_model), BF16)
        return 0

    lax.fori_loop(0, KERNEL, regroup, 0)

    def turn(block):
        return jnp.concatenate([block.astype(F32), pad_rows], 0).T

    @pl.when(me > 0)
    def _():
        pltpu.make_async_copy(recv_prev, recv_prev, prev_recv).wait()
        trans[pl.ds(16 + 128, 128)] = turn(recv_prev[...])

    for s in range(per_part):
        pltpu.make_async_copy(recv.at[s], recv.at[s], x_recv.at[s]).wait()
        for t in range(width // 128):
            trans[pl.ds(OWN_AT + s * width + t * 128, 128)] = turn(
                recv[s, :, pl.ds(t * 128, 128)]
            )

    if parts > 1:
        place = lax.rem(me, parts)

        @pl.when(place > 0)
        def _():
            trans[pl.ds(OWN_AT - 16, 4)] = trans[pl.ds(OWN_AT, 4)]
            trans[pl.ds(OWN_AT - 4, 4)] = trans[pl.ds(OWN_AT - 20, 4)]

        @pl.when(place < parts - 1)
        def _():
            pltpu.make_async_copy(recv_next, recv_next, next_recv).wait()
            trans[pl.ds(OWN_AT + per_part * width, 16)] = turn(recv_next[...])[0:16]

    for kx in range(KERNEL):
        lanes = pl.ds(kx * 128, 128)
        patches[pl.ds(0, LEAD), lanes] = trans[pl.ds(12 + kx, LEAD, stride=PATCH), :].astype(BF16)
        patches[pl.ds(LEAD, SPAN), lanes] = trans[
            pl.ds(OWN_AT - 4 + kx, SPAN, stride=PATCH), :
        ].astype(BF16)

    for n in range(d_model // 256):
        cs = pl.ds(n * 256, 256)
        acc = jnp.dot(patches[...], wp[:, cs], preferred_element_type=F32)
        emb[:, cs] = (acc + patch_b_ref[:, cs]).astype(BF16)
    resid = emb[...].astype(F32)
    mean_sq = jnp.mean(resid * resid, axis=-1, keepdims=True)
    normed[...] = (
        resid * lax.rsqrt(mean_sq + 1e-05) * norm_g_ref[...]
    ).astype(BF16)

    own = pl.ds(LEAD, SPAN)
    step_raw = lax.dot_general(
        normed[own], step_ref[...], (((1,), (1,)), ((), ())), preferred_element_type=F32
    )
    sx = step_raw + bias_ref[...]
    step = jax.nn.softplus(sx)
    log_decay = -step * jnp.exp(rate_ref[...])
    rows_i = lax.broadcasted_iota(jnp.int32, (SPAN, SPAN), 0)
    cols_i = lax.broadcasted_iota(jnp.int32, (SPAN, SPAN), 1)
    causal = rows_i >= cols_i
    cum = jnp.dot(causal.astype(F32), log_decay, precision=HI, preferred_element_type=F32)
    cum_last = cum[SPAN - 1 : SPAN, :]
    to_end = jnp.exp(cum_last - cum) * step
    unit = (
        lax.broadcasted_iota(jnp.int32, (HEADS, 128), 0)
        == lax.broadcasted_iota(jnp.int32, (HEADS, 128), 1)
    ).astype(F32)
    logs[me] = jnp.dot(
        jnp.broadcast_to(cum_last, (8, HEADS)), unit, precision=HI, preferred_element_type=F32
    )
    for hop in range(1, ndev):
        target = lax.rem(me + hop, ndev)
        sent.append(
            push(
                yes, logs.at[me], logs.at[me], l_send.at[hop], l_recv.at[hop], target
            )
        )

    loads[1].wait()
    total = mixw.shape[1]
    tiles = [(lo, min(256, total - lo)) for lo in range(0, total, 256)]
    has_prev = jnp.where(me > 0, 1.0, 0.0).astype(F32)
    for lo, size in tiles[::-1]:
        cs = pl.ds(lo, size)
        proj = jnp.dot(normed[...], mixw[:, cs], preferred_element_type=F32)
        raw[:, pl.ds(0, size)] = proj.astype(BF16).astype(F32)
        raw[pl.ds(0, LEAD), pl.ds(0, size)] = raw[pl.ds(0, LEAD), pl.ds(0, size)] * has_prev
        total_sum = conv_b_ref[:, cs]
        for k in range(4):
            total_sum = total_sum + tap_ref[pl.ds(k, 1), cs] * raw[
                pl.ds(LEAD - 3 + k, SPAN), pl.ds(0, size)
            ]
        mixed[:, cs] = jax.nn.silu(total_sum).astype(BF16)

    bc = mixed[:, pl.ds(E, 2 * NSTATE)]
    b_mat = bc[:, :NSTATE]
    c_mat = bc[:, NSTATE:]
    low_half = lax.broadcasted_iota(jnp.int32, (SPAN, 128), 1) < HDIM

    def spread(values, p):
        return jnp.where(
            low_half,
            jnp.broadcast_to(values[:, 2 * p : 2 * p + 1], (SPAN, 128)),
            jnp.broadcast_to(values[:, 2 * p + 1 : 2 * p + 2], (SPAN, 128)),
        )

    pairs = HEADS // 2
    for p in range(pairs):
        ps = pl.ds(p * 128, 128)
        xw[:, ps] = (mixed[:, ps].astype(F32) * spread(to_end, p)).astype(BF16)
    quart = E // 4
    for q in range(4):
        fresh = lax.dot_general(
            b_mat, xw[:, pl.ds(q * quart, quart)], (((0,), (0,)), ((), ())),
            preferred_element_type=F32,
        )
        squart[q] = fresh.astype(BF16)
    first = g * 4
    for hop in range(1, 4):
        other = lax.rem(e + hop, 4)
        sent.append(
            push(
                yes, squart.at[other], squart_in.at[hop - 1], q_send.at[hop], q_recv.at[hop],
                first + other,
            )
        )

    loads[2].wait()
    for n in range(E // 256):
        cs = pl.ds(n * 256, 256)
        gate[:, cs] = jnp.dot(normed[own], gatew[:, cs], preferred_element_type=F32).astype(BF16)
    scores = lax.dot_general(
        c_mat, b_mat, (((1,), (1,)), ((), ())), preferred_element_type=F32
    )
    cum_t = cum.T
    step_t = step.T

    def inside(p):
        ps = pl.ds(p * 128, 128)
        x = mixed[:, ps]
        ys = []
        for h in (2 * p, 2 * p + 1):
            gap = cum[:, h : h + 1] - cum_t[h : h + 1, :]
            decay = jnp.exp(jnp.where(causal, gap, -1e30))
            w = (scores * decay * step_t[h : h + 1, :]).astype(BF16)
            ys.append(jnp.dot(w, x, preferred_element_type=F32))
        skip = jnp.where(
            low_half, skip_ref[:, 2 * p : 2 * p + 1], skip_ref[:, 2 * p + 1 : 2 * p + 2]
        )
        yacc[:, ps] = jnp.where(low_half, ys[0], ys[1]) + skip * x.astype(F32)

    for p in range(0, 2):
        inside(p)

    for hop in range(1, ndev):
        source = lax.rem(me - hop + ndev, ndev)
        pltpu.make_async_copy(logs.at[source], logs.at[source], l_recv.at[hop]).wait()
    lanes_q = lax.broadcasted_iota(jnp.int32, (128, quart), 1) + e * quart
    pick = (lanes_q // HDIM == lax.broadcasted_iota(jnp.int32, (128, quart), 0)).astype(F32)

    def expand(tile):
        return jnp.exp(jnp.dot(tile, pick, precision=HI, preferred_element_type=F32))[0:1]

    for hop in range(1, 4):
        pltpu.make_async_copy(
            squart_in.at[hop - 1], squart_in.at[hop - 1], q_recv.at[hop]
        ).wait()
    prefix = [jnp.zeros((NSTATE, quart), F32)]
    befores = [jnp.zeros((8, 128), F32)]
    for n in range(4):
        hop = lax.rem(e - n + 4, 4)
        arrived = squart_in[jnp.maximum(hop - 1, 0)].astype(F32)
        state = jnp.where(hop == 0, squart[e].astype(F32), arrived)
        tile = logs[first + n]
        prefix.append(expand(tile) * prefix[-1] + state)
        befores.append(befores[-1] + tile)
    tot_out[...] = prefix[4].astype(BF16)
    for later in range(1, ngroup):
        sent.append(
            push(
                g < later, tot_out, tot_in.at[g], t_send.at[later], t_recv.at[g], later * 4 + e
            )
        )

    for p in range(2, 8):
        inside(p)

    inc_acc[...] = jnp.zeros_like(inc_acc)
    for k in range(ngroup - 1):

        @pl.when(k < g)
        def _():
            pltpu.make_async_copy(tot_in.at[k], tot_in.at[k], t_recv.at[k]).wait()
            tile = logs[4 * k] + logs[4 * k + 1] + logs[4 * k + 2] + logs[4 * k + 3]
            inc_acc[...] = expand(tile) * inc_acc[...] + tot_in[k].astype(F32)

    for n in range(4):
        inc_out[n] = (expand(befores[n]) * inc_acc[...] + prefix[n]).astype(BF16)
    for hop in range(1, 4):
        other = lax.rem(e + hop, 4)
        sent.append(
            push(
                yes, inc_out.at[other], inc_in.at[hop - 1], i_send.at[hop], i_recv.at[hop],
                first + other,
            )
        )
    for p in range(8, pairs):
        inside(p)
    for hop in range(1, 4):
        pltpu.make_async_copy(inc_in.at[hop - 1], inc_in.at[hop - 1], i_recv.at[hop]).wait()

    grown = jnp.exp(cum)
    sq = jnp.zeros((SPAN, 128), F32)
    for q in range(4):
        hop = lax.rem(e - q + 4, 4)
        incoming = jnp.where(hop == 0, inc_out[e], inc_in[jnp.maximum(hop - 1, 0)])
        ystate = jnp.dot(c_mat, incoming, preferred_element_type=F32)
        for n in range(quart // 128):
            p = q * (quart // 128) + n
            ps = pl.ds(p * 128, 128)
            y = yacc[:, ps] + ystate[:, n * 128 : n * 128 + 128] * spread(grown, p)
            y = y * jax.nn.silu(gate[:, ps].astype(F32))
            yacc[:, ps] = y
            sq = sq + y * y
    scale = lax.rsqrt(jnp.sum(sq, axis=-1, keepdims=True) / E + 1e-05)
    for p in range(pairs):
        ps = pl.ds(p * 128, 128)
        xw[:, ps] = (yacc[:, ps] * scale * gain_ref[:, ps]).astype(BF16)
    loads[3].wait()
    for n in range(d_model // 256):
        cs = pl.ds(n * 256, 256)
        acc = jnp.dot(xw[...], outw[:, cs], preferred_element_type=F32)
        o_ref[:, cs] = (acc + emb[own, cs].astype(F32)).astype(BF16)
    for done in sent:
        done()


def body(
    pixels, patch_weight, patch_bias, norm_gain, gate_weight, mix_weight, step_weight, step_bias,
    log_rate, conv_weight, conv_bias, skip_gain, out_gain, out_weight,
):
    cols = lax.axis_size("cols")
    nr = lax.axis_size("rows")
    chan, height, width = pixels.shape
    local_rows = height // PATCH
    ndev = cols * nr
    parts = ndev // (local_rows * nr)
    per_part = cols // parts
    ngroup = ndev // 4
    quart = E // 4
    d_model = patch_weight.shape[3]
    windows = jnp.pad(
        pixels.transpose(1, 0, 2).reshape(height * chan, width), ((16, 16), (0, 0))
    )
    wp = patch_weight.transpose(0, 2, 1, 3).reshape(KERNEL, CHAN * KERNEL, d_model)
    total = mix_weight.shape[1]

    hbm = pl.BlockSpec(memory_space=pl.ANY)
    vmem = pl.BlockSpec(memory_space=pltpu.VMEM)
    dma = pltpu.SemaphoreType.DMA
    tok = SPAN + LEAD
    return pl.pallas_call(
        functools.partial(layer_kernel, (cols, nr, local_rows, width)),
        out_shape=jax.ShapeDtypeStruct((SPAN, d_model), BF16),
        in_specs=[vmem, hbm, hbm, hbm, hbm] + [vmem] * 9,
        out_specs=vmem,
        scratch_shapes=[
            pltpu.VMEM(wp.shape, BF16),
            pltpu.VMEM((d_model // 128, 96 + KERNEL * CHAN * KERNEL + 96, 128), F32),
            pltpu.VMEM((KERNEL * 128, d_model), BF16),
            pltpu.VMEM(mix_weight.shape, BF16),
            pltpu.VMEM(gate_weight.shape, BF16),
            pltpu.VMEM(out_weight.shape, BF16),
            dma((4,)),
            pltpu.VMEM((per_part, WIN, width), BF16),
            pltpu.VMEM((WIN, 128), BF16),
            pltpu.VMEM((WIN, 128), BF16),
            pltpu.VMEM((OWN_AT + per_part * width + 16, 128), F32),
            pltpu.VMEM((tok, KERNEL * 128), BF16),
            pltpu.VMEM((tok, d_model), BF16),
            pltpu.VMEM((tok, d_model), BF16),
            pltpu.VMEM((tok, 256), F32),
            pltpu.VMEM((SPAN, total), BF16),
            pltpu.VMEM((SPAN, E), BF16),
            pltpu.VMEM((SPAN, E), F32),
            pltpu.VMEM((SPAN, E), BF16),
            pltpu.VMEM((4, NSTATE, quart), BF16),
            pltpu.VMEM((3, NSTATE, quart), BF16),
            pltpu.VMEM((ndev, 8, 128), F32),
            pltpu.VMEM((NSTATE, quart), BF16),
            pltpu.VMEM((ngroup, NSTATE, quart), BF16),
            pltpu.VMEM((4, NSTATE, quart), BF16),
            pltpu.VMEM((3, NSTATE, quart), BF16),
            pltpu.VMEM((NSTATE, quart), F32),
            dma((local_rows + 4,)),
            dma((local_rows + 4,)),
            dma((local_rows + 4,)),
            dma((per_part,)),
            dma,
            dma,
            dma((4,)),
            dma((4,)),
            dma((ndev,)),
            dma((ndev,)),
            dma((ngroup,)),
            dma((ngroup,)),
            dma((4,)),
            dma((4,)),
        ],
        compiler_params=pltpu.CompilerParams(
            collective_id=0, has_side_effects=True, vmem_limit_bytes=56 * 1024 * 1024
        ),
    )(
        windows, wp, mix_weight, gate_weight, out_weight, step_weight.T, conv_weight,
        conv_bias[None], out_gain[None], skip_gain[None], patch_bias[None], norm_gain[None],
        step_bias[None], log_rate[None],
    )


def solution(mesh):
    placed = (
        P(None, "rows", ("slides", "cols")),
        P(),
        P(),
        P(),
        P(),
        P(),
        P(),
        P(),
        P(),
        P(),
        P(),
        P(),
        P(),
        P(),
    )
    return jax.shard_map(
        body,
        mesh=mesh,
        in_specs=placed,
        out_specs=P(("slides", "cols", "rows"), None),
        check_vma=False,
    )
```
